32 devices in a mesh: uly: 4 (over y, x), blk: 8 (over z, core).
Axes of the slice: x: 2, y: 2, z: 4, core: 2. Of those that a mesh axis runs over, the one named last changes fastest.
Arguments:
- queries: bfloat16 [2048, 2048], P(('uly', 'blk')), may hold values from -6 to 6
- key_vector_rows: bfloat16 [2048, 256], P(('uly', 'blk')), may hold values from -6 to 6
- value_vector_rows: bfloat16 [2048, 256], P(('uly', 'blk')), may hold values from -6 to 6
- out_grad: bfloat16 [2048, 2048], P(('uly', 'blk')), may hold values from -6 to 6
- block_list: int32 [16, 16, 8], P('uly'), may hold values from 0 to 15, as said below
Outputs:
- attended: bfloat16 [2048, 2048], P(('uly', 'blk'))
- query_grad: bfloat16 [2048, 2048], P(('uly', 'blk'))
- gradient_keys: bfloat16 [2048, 256], P(('uly', 'blk'))
- gradient_values: bfloat16 [2048, 256], P(('uly', 'blk'))
The draws below stay inside these ranges and needn't reach their ends.
Inputs may be any that keep to these rules, and one draw needn't show every extreme that they name: block_list[h, i] names key blocks for query block i of head h: its first entry is always i itself, every entry is at most i, and a block may be named several times.
All inputs are finite; a program needn't handle non-finite values.
Results may differ from the reference program's by a relative error of at most 0.039.
Values may be sent and summed in bfloat16 or wider, within the bound.
A program may use at most 128 MiB of HBM per device.

```python
import math
import jax
import jax.numpy as jnp
from jax import lax

QUERY_HEADS = 16
KEY_VALUE_HEADS = 2
HEAD_SIZE = 128
BLOCK = 128
KMAX = 8
SEQUENCE_TOKENS = 2048
NB = 16


def draw_queries(key, part):
    sampled_values = jax.random.normal(jax.random.fold_in(key, 21), (SEQUENCE_TOKENS, QUERY_HEADS, HEAD_SIZE), jnp.float32)
    return jnp.clip(sampled_values, -6.0, 6.0).reshape(SEQUENCE_TOKENS, QUERY_HEADS * HEAD_SIZE).astype(jnp.bfloat16)


def draw_key_vector_rows(key, part):
    sampled_values = jax.random.normal(jax.random.fold_in(key, 22), (SEQUENCE_TOKENS, KEY_VALUE_HEADS, HEAD_SIZE), jnp.float32)
    return jnp.clip(sampled_values, -6.0, 6.0).reshape(SEQUENCE_TOKENS, KEY_VALUE_HEADS * HEAD_SIZE).astype(jnp.bfloat16)


def draw_block_list(key, part):
    first_key = jax.random.fold_in(key, 31)
    second_key = jax.random.fold_in(key, 32)
    third_key = jax.random.fold_in(key, 33)
    row_ids = jnp.arange(NB, dtype=jnp.int32)[:, None]
    col_ids = jnp.arange(NB, dtype=jnp.int32)[None, :]
    ranking = jax.random.randint(first_key, (QUERY_HEADS, NB, NB), 0, 1 << 20) * NB + col_ids
    ranking = jnp.where(col_ids == row_ids, 1 << 30, ranking)
    ranking = jnp.where(col_ids > row_ids, -1 - col_ids, ranking)
    chosen = lax.top_k(ranking, KMAX)[1].astype(jnp.int32)
    head_cap = jax.random.randint(second_key, (QUERY_HEADS, 1), 2, KMAX + 1)
    counts = jax.random.randint(third_key, (QUERY_HEADS, NB), 1, KMAX + 1)
    counts = jnp.minimum(jnp.minimum(counts, head_cap), row_ids[:, 0][None, :] + 1)
    slot_ids = jnp.arange(KMAX, dtype=jnp.int32)
    diagonal = jnp.broadcast_to(row_ids[None, :, :], (QUERY_HEADS, NB, KMAX))
    return jnp.where(slot_ids[None, None, :] < counts[:, :, None], chosen, diagonal).astype(jnp.int32)


def level_of(key, shape, shards, smallest, top_value):
    factor_of = 1.0
    for axis_at, blocks in shards:
        steps = jax.random.uniform(jax.random.fold_in(jax.random.fold_in(key, 6), axis_at), (blocks,), jnp.float32, smallest / len(shards), top_value / len(shards))
        factor_of = factor_of * jnp.repeat(jnp.exp(steps), shape[axis_at] // blocks).reshape((-1,) + (1,) * (len(shape) - 1 - axis_at))
    return factor_of


def centred(key, dims, width, limit, cuts=(), kind=jnp.bfloat16):
    level = level_of(key, dims, cuts, -0.22, 0.18) if cuts else 1.0
    result = jax.random.normal(key, dims, jnp.float32) * width * level
    return jnp.minimum(jnp.maximum(result, -limit), limit).astype(kind)


def setup_inputs(seed: int = 0) -> dict:
    seeds = jax.random.split(jax.random.key(seed), 6)
    return {
        "queries": draw_queries(jax.random.fold_in(seeds[5], 71), 0),
        "key_vector_rows": draw_key_vector_rows(jax.random.fold_in(seeds[5], 71), 0),
        "value_vector_rows": centred(seeds[2], (SEQUENCE_TOKENS, KEY_VALUE_HEADS * HEAD_SIZE), 1.0, 6.0, ((0, 32),)),
        "out_grad": centred(seeds[3], (SEQUENCE_TOKENS, QUERY_HEADS * HEAD_SIZE), 1.0, 6.0, ((0, 32),)),
        "block_list": draw_block_list(jax.random.fold_in(seeds[5], 71), 0),
    }


def head_pass(head_index, queries3, keys_by_head, values_by_head, grads3, block_list):
    query_group_width = QUERY_HEADS // KEY_VALUE_HEADS
    query_head = queries3[head_index]
    key_head = keys_by_head[head_index // query_group_width]
    value_head = values_by_head[head_index // query_group_width]
    grad_head = grads3[head_index]
    lists_head = block_list[head_index]
    score_scale = 1.0 / math.sqrt(HEAD_SIZE)
    offsets = jnp.arange(BLOCK, dtype=jnp.int32)
    earlier = jnp.arange(KMAX)[:, None] > jnp.arange(KMAX)[None, :]

    def block_step(sums_pair, block_index):
        key_acc, value_acc = sums_pair
        first_row = block_index * BLOCK
        query_block = lax.dynamic_slice_in_dim(query_head, first_row, BLOCK, 0)
        grad_block = lax.dynamic_slice_in_dim(grad_head, first_row, BLOCK, 0)
        entries = lists_head[block_index]
        repeated = jnp.any((entries[:, None] == entries[None, :]) & earlier, axis=1)
        positions = (entries[:, None] * BLOCK + offsets[None, :]).reshape(-1).astype(jnp.int32)
        live_keys = jnp.repeat(jnp.logical_not(repeated), BLOCK)
        query_pos = first_row + offsets
        allowed = (positions[None, :] <= query_pos[:, None]) & live_keys[None, :]
        key_block = key_head[positions]
        value_block = value_head[positions]
        scores = jnp.dot(query_block, key_block.T, preferred_element_type=jnp.float32) * score_scale
        masked = jnp.where(allowed, scores, -1e+30)
        row_max = lax.optimization_barrier(jnp.max(masked, axis=1, keepdims=True))
        row_sum = lax.optimization_barrier(jnp.sum(jnp.where(allowed, jnp.exp(masked - row_max), 0.0), axis=1, keepdims=True))
        log_sum = row_max + jnp.log(row_sum)
        weights = jnp.where(allowed, jnp.exp(masked - log_sum), 0.0)
        weights_low = weights.astype(jnp.bfloat16)
        out_block = jnp.dot(weights_low, value_block, preferred_element_type=jnp.float32).astype(jnp.bfloat16)
        row_dot = lax.optimization_barrier(jnp.sum(grad_block.astype(jnp.float32) * out_block.astype(jnp.float32), axis=1, keepdims=True))
        grad_weights = jnp.dot(grad_block, value_block.T, preferred_element_type=jnp.float32)
        score_grad = (weights * (grad_weights - row_dot) * score_scale).astype(jnp.bfloat16)
        query_block_grad = jnp.dot(score_grad, key_block, preferred_element_type=jnp.float32).astype(jnp.bfloat16)
        key_acc = key_acc.at[positions].add(jnp.dot(score_grad.T, query_block, preferred_element_type=jnp.float32))
        value_acc = value_acc.at[positions].add(jnp.dot(weights_low.T, grad_block, preferred_element_type=jnp.float32))
        return ((key_acc, value_acc), (out_block, query_block_grad))
    empty_grad = jnp.zeros((SEQUENCE_TOKENS, HEAD_SIZE), jnp.float32)
    sums_pair, outputs = lax.scan(block_step, (empty_grad, empty_grad), jnp.arange(NB, dtype=jnp.int32))
    return (outputs[0].reshape(SEQUENCE_TOKENS, HEAD_SIZE), outputs[1].reshape(SEQUENCE_TOKENS, HEAD_SIZE), sums_pair[0], sums_pair[1])

def reference(queries, key_vector_rows, value_vector_rows, out_grad, block_list):
    queries3 = queries.reshape(SEQUENCE_TOKENS, QUERY_HEADS, HEAD_SIZE).transpose(1, 0, 2)
    grads3 = out_grad.reshape(SEQUENCE_TOKENS, QUERY_HEADS, HEAD_SIZE).transpose(1, 0, 2)
    keys_by_head = key_vector_rows.reshape(SEQUENCE_TOKENS, KEY_VALUE_HEADS, HEAD_SIZE).transpose(1, 0, 2)
    values_by_head = value_vector_rows.reshape(SEQUENCE_TOKENS, KEY_VALUE_HEADS, HEAD_SIZE).transpose(1, 0, 2)

    def per_head(head_index):
        return head_pass(head_index, queries3, keys_by_head, values_by_head, grads3, block_list)
    attended, query_grad, key_portion, value_portion = lax.map(per_head, jnp.arange(QUERY_HEADS, dtype=jnp.int32))
    attended = attended.transpose(1, 0, 2).reshape(SEQUENCE_TOKENS, QUERY_HEADS * HEAD_SIZE)
    query_grad = query_grad.transpose(1, 0, 2).reshape(SEQUENCE_TOKENS, QUERY_HEADS * HEAD_SIZE)
    gradient_keys = key_portion.reshape(KEY_VALUE_HEADS, QUERY_HEADS // KEY_VALUE_HEADS, SEQUENCE_TOKENS, HEAD_SIZE).sum(axis=1).transpose(1, 0, 2).reshape(SEQUENCE_TOKENS, KEY_VALUE_HEADS * HEAD_SIZE).astype(jnp.bfloat16)
    gradient_values = value_portion.reshape(KEY_VALUE_HEADS, QUERY_HEADS // KEY_VALUE_HEADS, SEQUENCE_TOKENS, HEAD_SIZE).sum(axis=1).transpose(1, 0, 2).reshape(SEQUENCE_TOKENS, KEY_VALUE_HEADS * HEAD_SIZE).astype(jnp.bfloat16)
    return (attended, query_grad, gradient_keys, gradient_values)
```

```python
import functools
import math

import jax
import jax.numpy as jnp
from jax import lax
from jax.experimental import pallas as pl
from jax.experimental.pallas import tpu as pltpu
from jax.sharding import PartitionSpec as P

KEY_VALUE_HEADS = 2
HEAD_SIZE = 128
BLOCK = 128
MESH = pl.DeviceIdType.MESH
VMEM_LIMIT = 56 * 1024 * 1024


def flip(u, mask, width):
    bit = 1
    while bit < width:
        if mask & bit:
            u = u + bit * (1 - 2 * ((u // bit) % 2))
        bit *= 2
    return u


def bits_of(width):
    return [1 << t for t in range(width.bit_length() - 1)]


def span(bits):
    masks = [0]
    for bit in bits:
        masks = masks + [m | bit for m in masks]
    return masks


def greet(width, chips, u, b, c, g):
    barrier = pltpu.get_barrier_semaphore()
    peers = [(u, c * 2 + (1 - g))]
    peers += [(u, ((c + d) % chips) * 2 + g) for d in range(1, chips)]
    peers += [(flip(u, m, width), b) for m in range(1, width)]
    for peer in peers:
        pl.semaphore_signal(barrier, inc=1, device_id=peer, device_id_type=MESH)
    pl.semaphore_wait(barrier, len(peers))


def remote(src, dst, send_sem, recv_sem, device):
    return pltpu.make_async_remote_copy(
        src_ref=src, dst_ref=dst, send_sem=send_sem, recv_sem=recv_sem,
        device_id=device, device_id_type=MESH,
    )


def gather_kernel(
    width, chips,
    q_ref, do_ref, k_ref, v_ref, list_ref,
    qx, dox, kall, vall, kt, vt, table,
    ks, kr, vs, vr, ts, tr, ps, pr,
):
    u, b = lax.axis_index("uly"), lax.axis_index("blk")
    c, g = b // 2, b % 2
    half = q_ref.shape[1] // 2
    seg = q_ref.shape[0]
    me = u * chips + c
    mine = pl.ds(pl.multiple_of(g * seg, seg), seg)
    my_head = pl.ds(pl.multiple_of(g * HEAD_SIZE, HEAD_SIZE), HEAD_SIZE)
    other_head = pl.ds(pl.multiple_of((1 - g) * HEAD_SIZE, HEAD_SIZE), HEAD_SIZE)
    my_half = pl.ds(pl.multiple_of(g * half, half), half)
    other_half = pl.ds(pl.multiple_of((1 - g) * half, half), half)
    sibling = (u, c * 2 + (1 - g))

    kall[me, mine, :] = k_ref[:, my_head]
    vall[me, mine, :] = v_ref[:, my_head]
    table[u] = list_ref[...]
    greet(width, chips, u, b, c, g)

    started = []

    def start(copy):
        copy.start()
        started.append(copy)
        return copy

    pair = [
        start(remote(k_ref.at[:, other_head], kall.at[me, mine, :], ps.at[0], pr.at[0], sibling)),
        start(remote(v_ref.at[:, other_head], vall.at[me, mine, :], ps.at[1], pr.at[1], sibling)),
        start(remote(q_ref.at[:, other_half], qx.at[mine, :], ps.at[2], pr.at[2], sibling)),
        start(remote(do_ref.at[:, other_half], dox.at[mine, :], ps.at[3], pr.at[3], sibling)),
    ]
    tables = [
        start(remote(list_ref, table.at[u], ts.at[m], tr.at[m], (flip(u, m, width), b)))
        for m in range(1, width)
    ]
    qx[mine, :] = q_ref[:, my_half]
    dox[mine, :] = do_ref[:, my_half]

    def place(m, d):
        return flip(u, m, width) * chips + (c + d) % chips

    orders = (bits_of(width), bits_of(width)[::-1])
    arrays = ((kall, ks, kr, kt), (vall, vs, vr, vt))

    def forward(which, m, d):
        ref, send, recv, _ = arrays[which]
        order = orders[which]
        at = place(m, d)
        if m == 0 and d == 0:
            for e in range(1, chips):
                peer = (u, ((c + e) % chips) * 2 + g)
                start(remote(ref.at[at], ref.at[at], send.at[e], recv.at[(chips - e) % chips], peer))
        last = max([t for t, bit in enumerate(order) if m & bit], default=-1)
        for bit in order[last + 1:]:
            slot = (m ^ bit) * chips + d
            peer = (flip(u, bit, width), b)
            start(remote(ref.at[at], ref.at[at], send.at[slot], recv.at[slot], peer))

    def arrived(which, m, d):
        ref, send, recv, _ = arrays[which]
        at = place(m, d)
        slot = m * chips + d
        remote(ref.at[at], ref.at[at], send.at[slot], recv.at[slot], sibling).wait_recv()

    def turn(which, m, d):
        ref, _, _, turned = arrays[which]
        at = place(m, d)
        turned[at] = ref[at].T

    items = sorted(
        ((m, d) for m in range(width) for d in range(chips)),
        key=lambda item: (item[1] + 1.1 * bin(item[0]).count("1"), item[0]),
    )
    pair[0].wait_recv()
    forward(0, 0, 0)
    pair[1].wait_recv()
    forward(1, 0, 0)
    turn(0, 0, 0)
    turn(1, 0, 0)
    for m, d in items:
        if m == 0 and d == 0:
            continue
        for which in (0, 1):
            arrived(which, m, d)
            forward(which, m, d)
        for which in (0, 1):
            turn(which, m, d)
    pair[2].wait_recv()
    pair[3].wait_recv()
    for copy in tables:
        copy.wait_recv()
    for copy in started:
        copy.wait_send()


def attention_kernel(
    chips, heads, list_len,
    table, qx, dox, kall, vall, kt, vt,
    outx, dqx, gk, gv,
    names, kacc, vacc,
):
    u, b = lax.axis_index("uly"), lax.axis_index("blk")
    g = b % 2
    block = u * chips + b // 2
    blocks = kall.shape[0]
    per_shard = table.shape[1]
    scale = 1.0 / math.sqrt(HEAD_SIZE)
    log2e = math.log2(math.e)

    def clear(j, carry):
        kacc[j] = jnp.zeros((BLOCK, HEAD_SIZE), jnp.float32)
        vacc[j] = jnp.zeros((BLOCK, HEAD_SIZE), jnp.float32)
        return carry

    lax.fori_loop(0, blocks, clear, 0)

    def work(n, columns):
        at = [names[t] for t in range(n)]
        q = qx[:, columns]
        do = dox[:, columns]
        keys = jnp.concatenate([kall[e] for e in at], axis=0)
        values = jnp.concatenate([vall[e] for e in at], axis=0)
        contract = (((1,), (1,)), ((), ()))
        scores = lax.dot_general(keys, q, contract, preferred_element_type=jnp.float32)
        scores = scores * (scale * log2e)
        row = lax.broadcasted_iota(jnp.int32, (BLOCK, BLOCK), 0)
        col = lax.broadcasted_iota(jnp.int32, (BLOCK, BLOCK), 1)
        head_part = jnp.where(row <= col, scores[:BLOCK], -1e30)
        scores = jnp.concatenate([head_part, scores[BLOCK:]], axis=0) if n > 1 else head_part
        top = jnp.max(scores, axis=0, keepdims=True)
        powers = jnp.exp2(scores - top)
        weights = powers * (1.0 / jnp.sum(powers, axis=0, keepdims=True))
        low = weights.astype(jnp.bfloat16)
        grad_weights = lax.dot_general(values, do, contract, preferred_element_type=jnp.float32)
        row_dot = jnp.sum(weights * grad_weights, axis=0, keepdims=True)
        score_grad = (weights * (grad_weights - row_dot) * scale).astype(jnp.bfloat16)
        values_t = jnp.concatenate([vt[e] for e in at], axis=1)
        keys_t = jnp.concatenate([kt[e] for e in at], axis=1)
        out_t = jnp.dot(values_t, low, preferred_element_type=jnp.float32)
        dq_t = jnp.dot(keys_t, score_grad, preferred_element_type=jnp.float32)
        outx[:, columns] = out_t.T.astype(jnp.bfloat16)
        dqx[:, columns] = dq_t.T.astype(jnp.bfloat16)
        dv = jnp.dot(low, do, preferred_element_type=jnp.float32)
        dk = jnp.dot(score_grad, q, preferred_element_type=jnp.float32)
        for t, e in enumerate(at):
            kacc[e] += dk[t * BLOCK:(t + 1) * BLOCK]
            vacc[e] += dv[t * BLOCK:(t + 1) * BLOCK]

    def head_step(h, carry):
        head = g * heads + h
        shard, local = head // per_shard, head % per_shard
        count = jnp.int32(1)
        names[0] = block
        for t in range(1, list_len):
            entry = table[shard, local, block * list_len + t]
            names[count] = entry
            count = count + jnp.where(entry < blocks, 1, 0).astype(jnp.int32)
        columns = pl.ds(pl.multiple_of(h * HEAD_SIZE, HEAD_SIZE), HEAD_SIZE)
        for n in range(1, list_len + 1):
            pl.when(count == n)(functools.partial(work, n, columns))
        return carry

    lax.fori_loop(0, heads, head_step, 0)

    def finish(j, carry):
        gk[j] = kacc[j].astype(jnp.bfloat16)
        gv[j] = vacc[j].astype(jnp.bfloat16)
        return carry

    lax.fori_loop(0, blocks, finish, 0)


def scatter_kernel(
    width, chips,
    outx, dqx, gk, gv,
    out, dq, out_k, out_v,
    rk, rv, ak, av, fk, fv,
    ks, kr, vs, vr, ps, pr,
):
    u, b = lax.axis_index("uly"), lax.axis_index("blk")
    c, g = b // 2, b % 2
    half = outx.shape[1]
    seg = out.shape[0]
    mine = pl.ds(pl.multiple_of(g * seg, seg), seg)
    theirs = pl.ds(pl.multiple_of((1 - g) * seg, seg), seg)
    my_head = pl.ds(pl.multiple_of(g * HEAD_SIZE, HEAD_SIZE), HEAD_SIZE)
    my_half = pl.ds(pl.multiple_of(g * half, half), half)
    sibling = (u, c * 2 + (1 - g))
    greet(width, chips, u, b, c, g)
    started = []

    def start(copy):
        copy.start()
        started.append(copy)
        return copy

    def place(m, d):
        return flip(u, m, width) * chips + (c + d) % chips

    orders = (bits_of(width)[::-1], bits_of(width))
    arrays = ((gk, rk, ak, ks, kr), (gv, rv, av, vs, vr))
    stages = len(orders[0])
    bases = []
    total = 0
    for t in range(stages):
        bases.append(total)
        total += (width >> (t + 1)) * chips
    line = total
    ranked = [
        [sorted(span(order[t + 1:]), key=lambda m: -bin(m).count("1")) for t in range(stages)]
        for order in orders
    ]

    def slot(which, t, s, d):
        return bases[t] + ranked[which][t].index(s) * chips + d

    def current(which, t, m, d):
        grads, _, sums, _, _ = arrays[which]
        if t == 0:
            return grads.at[place(m, d)]
        return sums.at[slot(which, t - 1, m, d)]

    def send(which, t, s, d):
        _, landing, _, ssem, rsem = arrays[which]
        bit = orders[which][t]
        at = slot(which, t, s, d)
        start(remote(
            current(which, t, s ^ bit, d), landing.at[at], ssem.at[at], rsem.at[at],
            (flip(u, bit, width), b),
        ))

    line_order = list(range(1, chips)) + [0]
    for t_s in range(width // 2):
        for d in line_order:
            for which in (0, 1):
                send(which, 0, ranked[which][0][t_s], d)
    pair = [
        start(remote(outx.at[theirs, :], out.at[:, my_half], ps.at[0], pr.at[0], sibling)),
        start(remote(dqx.at[theirs, :], dq.at[:, my_half], ps.at[1], pr.at[1], sibling)),
    ]
    out[:, my_half] = outx[mine, :]
    dq[:, my_half] = dqx[mine, :]

    for t in range(stages):
        for s_at in range(len(ranked[0][t])):
            for d in line_order:
                for which in (0, 1):
                    _, landing, sums, ssem, rsem = arrays[which]
                    s = ranked[which][t][s_at]
                    at = slot(which, t, s, d)
                    remote(
                        landing.at[at], landing.at[at], ssem.at[at], rsem.at[at], sibling
                    ).wait_recv()
                    own = current(which, t, s, d)
                    sums[at] = (
                        own[...].astype(jnp.float32) + landing[at].astype(jnp.float32)
                    ).astype(jnp.bfloat16)
                    if t + 1 < stages:
                        if s & orders[which][t + 1]:
                            send(which, t + 1, s ^ orders[which][t + 1], d)
                    elif d:
                        start(remote(
                            sums.at[at], landing.at[line + (chips - d) % chips],
                            ssem.at[line + d], rsem.at[line + (chips - d) % chips],
                            (u, ((c + d) % chips) * 2 + g),
                        ))
    finals = ((fk, out_k), (fv, out_v))
    last = []
    for which in (0, 1):
        _, landing, sums, ssem, rsem = arrays[which]
        result, target = finals[which]
        value = sums[slot(which, stages - 1, 0, 0)].astype(jnp.float32)
        for d in range(1, chips):
            at = line + d
            remote(landing.at[at], landing.at[at], ssem.at[at], rsem.at[at], sibling).wait_recv()
            value = value + landing[at].astype(jnp.float32)
        result[...] = value.astype(jnp.bfloat16)
        last.append(start(remote(
            result.at[theirs, :], target.at[:, my_head], ps.at[2 + which], pr.at[2 + which], sibling
        )))
        target[:, my_head] = result[mine, :]
    for copy in pair + last:
        copy.wait_recv()
    for copy in started:
        copy.wait_send()


def body(queries, key_rows, value_rows, out_grad, block_list):
    width = lax.axis_size("uly")
    chips = lax.axis_size("blk") // 2
    seg, columns = queries.shape
    heads_dev, blocks, list_len = block_list.shape
    heads = heads_dev * width // KEY_VALUE_HEADS
    half = columns // 2
    low = jnp.bfloat16
    vmem = pl.BlockSpec(memory_space=pltpu.VMEM)
    smem = pl.BlockSpec(memory_space=pltpu.SMEM)
    dma = pltpu.SemaphoreType.DMA

    earlier = jnp.arange(list_len)[:, None] > jnp.arange(list_len)[None, :]
    repeated = jnp.any(
        (block_list[:, :, :, None] == block_list[:, :, None, :]) & earlier[None, None], axis=3
    )
    lists = jnp.where(repeated, blocks, block_list).reshape(heads_dev, blocks * list_len)

    cube = jax.ShapeDtypeStruct((blocks, BLOCK, HEAD_SIZE), low)
    wide = jax.ShapeDtypeStruct((BLOCK, half), low)
    qx, dox, kall, vall, kt, vt, table = pl.pallas_call(
        functools.partial(gather_kernel, width, chips),
        out_shape=(
            wide, wide, cube, cube, cube, cube,
            jax.ShapeDtypeStruct((width, heads_dev, blocks * list_len), jnp.int32),
        ),
        in_specs=[vmem] * 5,
        out_specs=(vmem,) * 7,
        scratch_shapes=[dma((width * chips,))] * 4 + [dma((width,))] * 2 + [dma((4,))] * 2,
        compiler_params=pltpu.CompilerParams(
            collective_id=0, has_side_effects=True, vmem_limit_bytes=VMEM_LIMIT
        ),
        name="gather",
    )(queries, out_grad, key_rows, value_rows, lists)

    outx, dqx, gk, gv = pl.pallas_call(
        functools.partial(attention_kernel, chips, heads, list_len),
        out_shape=(wide, wide, cube, cube),
        in_specs=[smem] + [vmem] * 6,
        out_specs=(vmem,) * 4,
        scratch_shapes=[
            pltpu.SMEM((list_len + 1,), jnp.int32),
            pltpu.VMEM((blocks, BLOCK, HEAD_SIZE), jnp.float32),
            pltpu.VMEM((blocks, BLOCK, HEAD_SIZE), jnp.float32),
        ],
        compiler_params=pltpu.CompilerParams(vmem_limit_bytes=VMEM_LIMIT),
        name="attention",
    )(table, qx, dox, kall, vall, kt, vt)

    slots = width * chips
    landing = pltpu.VMEM((slots, BLOCK, HEAD_SIZE), low)
    return pl.pallas_call(
        functools.partial(scatter_kernel, width, chips),
        out_shape=(
            jax.ShapeDtypeStruct((seg, columns), low),
            jax.ShapeDtypeStruct((seg, columns), low),
            jax.ShapeDtypeStruct((seg, KEY_VALUE_HEADS * HEAD_SIZE), low),
            jax.ShapeDtypeStruct((seg, KEY_VALUE_HEADS * HEAD_SIZE), low),
        ),
        in_specs=[vmem] * 4,
        out_specs=(vmem,) * 4,
        scratch_shapes=[landing] * 4
        + [pltpu.VMEM((BLOCK, HEAD_SIZE), low)] * 2
        + [dma((slots,))] * 4
        + [dma((4,))] * 2,
        compiler_params=pltpu.CompilerParams(
            collective_id=1, has_side_effects=True, vmem_limit_bytes=VMEM_LIMIT
        ),
        name="scatter",
    )(outx, dqx, gk, gv)


def solution(mesh):
    rows = P(("uly", "blk"), None)
    return jax.shard_map(
        body,
        mesh=mesh,
        in_specs=(rows, rows, rows, rows, P("uly", None, None)),
        out_specs=(rows, rows, rows, rows),
        check_vma=False,
    )
```

```python
import functools
import math

import jax
import jax.numpy as jnp
from jax import lax
from jax.experimental import pallas as pl
from jax.experimental.pallas import tpu as pltpu
from jax.sharding import PartitionSpec as P

KEY_VALUE_HEADS = 2
HEAD_SIZE = 128
BLOCK = 128
MESH = pl.DeviceIdType.MESH
VMEM_LIMIT = 56 * 1024 * 1024


def flip(u, mask, width):
    bit = 1
    while bit < width:
        if mask & bit:
            u = u + bit * (1 - 2 * ((u // bit) % 2))
        bit *= 2
    return u


def top(u, bits):
    for bit in bits:
        u = u + bit * (1 - (u // bit) % 2)
    return u


def bits_of(width):
    return [1 << t for t in range(width.bit_length() - 1)]


def span(bits):
    masks = [0]
    for bit in bits:
        masks = masks + [m | bit for m in masks]
    return masks


def greet(width, chips, u, b, c, g):
    barrier = pltpu.get_barrier_semaphore()
    peers = [(u, c * 2 + (1 - g))]
    peers += [(u, ((c + d) % chips) * 2 + g) for d in range(1, chips)]
    peers += [(flip(u, m, width), b) for m in range(1, width)]
    for peer in peers:
        pl.semaphore_signal(barrier, inc=1, device_id=peer, device_id_type=MESH)
    pl.semaphore_wait(barrier, len(peers))


def remote(src, dst, send_sem, recv_sem, device):
    return pltpu.make_async_remote_copy(
        src_ref=src, dst_ref=dst, send_sem=send_sem, recv_sem=recv_sem,
        device_id=device, device_id_type=MESH,
    )


def gather_kernel(
    width, chips,
    q_ref, do_ref, k_ref, v_ref, list_ref,
    qx, dox, kall, vall, kt, vt, table,
    ks, kr, vs, vr, ts, tr, ps, pr,
):
    u, b = lax.axis_index("uly"), lax.axis_index("blk")
    c, g = b // 2, b % 2
    half = q_ref.shape[1] // 2
    seg = q_ref.shape[0]
    me = u * chips + c
    mine = pl.ds(pl.multiple_of(g * seg, seg), seg)
    my_head = pl.ds(pl.multiple_of(g * HEAD_SIZE, HEAD_SIZE), HEAD_SIZE)
    other_head = pl.ds(pl.multiple_of((1 - g) * HEAD_SIZE, HEAD_SIZE), HEAD_SIZE)
    my_half = pl.ds(pl.multiple_of(g * half, half), half)
    other_half = pl.ds(pl.multiple_of((1 - g) * half, half), half)
    sibling = (u, c * 2 + (1 - g))

    kall[me, mine, :] = k_ref[:, my_head]
    vall[me, mine, :] = v_ref[:, my_head]
    table[u] = list_ref[...]
    greet(width, chips, u, b, c, g)

    started = []

    def start(copy, needed=None):
        if needed is None:
            copy.start()
        else:
            pl.when(needed)(copy.start)
        started.append((copy, needed))
        return copy

    pair = [
        start(remote(k_ref.at[:, other_head], kall.at[me, mine, :], ps.at[0], pr.at[0], sibling)),
        start(remote(v_ref.at[:, other_head], vall.at[me, mine, :], ps.at[1], pr.at[1], sibling)),
    ]

    def place(m, d):
        return flip(u, m, width) * chips + (c + d) % chips

    orders = (bits_of(width), bits_of(width)[::-1])
    arrays = ((kall, ks, kr, kt), (vall, vs, vr, vt))

    def later(which, m):
        order = orders[which]
        return order[max([t for t, bit in enumerate(order) if m & bit], default=-1) + 1:]

    def wanted(which, m, d):
        return place(m, d) <= top(u, later(which, m)) * chips + c

    def forward(which, m, d):
        ref, send, recv, _ = arrays[which]
        at = place(m, d)
        if m == 0 and d == 0:
            for e in range(1, chips):
                there = (c + e) % chips
                start(
                    remote(
                        ref.at[at], ref.at[at], send.at[e], recv.at[(chips - e) % chips],
                        (u, there * 2 + g),
                    ),
                    at <= (width - 1) * chips + there,
                )
        for bit in later(which, m):
            slot = (m ^ bit) * chips + d
            u_there = flip(u, bit, width)
            start(
                remote(ref.at[at], ref.at[at], send.at[slot], recv.at[slot], (u_there, b)),
                at <= top(u_there, later(which, m ^ bit)) * chips + c,
            )

    def arrived(which, m, d):
        ref, send, recv, _ = arrays[which]
        at = place(m, d)
        slot = m * chips + d
        copy = remote(ref.at[at], ref.at[at], send.at[slot], recv.at[slot], sibling)
        pl.when(wanted(which, m, d))(copy.wait_recv)

    def turn(which, m, d):
        ref, _, _, turned = arrays[which]
        at = place(m, d)

        @pl.when(at <= me)
        def _():
            turned[at] = ref[at].T

    items = [
        (which, m, d)
        for m in range(width) for d in range(chips) for which in (0, 1)
        if (m, d) != (0, 0)
    ]
    items.sort(key=lambda item: (
        not later(item[0], item[1]), item[2] + 1.1 * bin(item[1]).count("1")
    ))
    pair[0].wait_recv()
    forward(0, 0, 0)
    pair[1].wait_recv()
    forward(1, 0, 0)
    pair += [
        start(remote(q_ref.at[:, other_half], qx.at[mine, :], ps.at[2], pr.at[2], sibling)),
        start(remote(do_ref.at[:, other_half], dox.at[mine, :], ps.at[3], pr.at[3], sibling)),
    ]
    tables = [
        start(remote(list_ref, table.at[u], ts.at[m], tr.at[m], (flip(u, m, width), b)))
        for m in range(1, width)
    ]
    qx[mine, :] = q_ref[:, my_half]
    dox[mine, :] = do_ref[:, my_half]
    handed_on = [item for item in items if later(item[0], item[1])]
    for item in handed_on:
        arrived(*item)
        forward(*item)
    for which in (0, 1):
        turn(which, 0, 0)
    for item in handed_on:
        turn(*item)
    for item in items[len(handed_on):]:
        arrived(*item)
        turn(*item)
    pair[2].wait_recv()
    pair[3].wait_recv()
    for copy in tables:
        copy.wait_recv()
    for copy, needed in started:
        if needed is None:
            copy.wait_send()
        else:
            pl.when(needed)(copy.wait_send)


def attention_kernel(
    chips, heads, list_len,
    table, qx, dox, kall, vall, kt, vt,
    outx, dqx, gk, gv,
    names, kacc, vacc,
):
    u, b = lax.axis_index("uly"), lax.axis_index("blk")
    g = b % 2
    block = u * chips + b // 2
    blocks = kall.shape[0]
    per_shard = table.shape[1]
    scale = 1.0 / math.sqrt(HEAD_SIZE)
    log2e = math.log2(math.e)

    def clear(j, carry):
        kacc[j] = jnp.zeros((BLOCK, HEAD_SIZE), jnp.float32)
        vacc[j] = jnp.zeros((BLOCK, HEAD_SIZE), jnp.float32)
        return carry

    lax.fori_loop(0, blocks, clear, 0)

    def work(n, columns):
        at = [names[t] for t in range(n)]
        q = qx[:, columns]
        do = dox[:, columns]
        keys = jnp.concatenate([kall[e] for e in at], axis=0)
        values = jnp.concatenate([vall[e] for e in at], axis=0)
        contract = (((1,), (1,)), ((), ()))
        scores = lax.dot_general(keys, q, contract, preferred_element_type=jnp.float32)
        scores = scores * (scale * log2e)
        row = lax.broadcasted_iota(jnp.int32, (BLOCK, BLOCK), 0)
        col = lax.broadcasted_iota(jnp.int32, (BLOCK, BLOCK), 1)
        head_part = jnp.where(row <= col, scores[:BLOCK], -1e30)
        scores = jnp.concatenate([head_part, scores[BLOCK:]], axis=0) if n > 1 else head_part
        top = jnp.max(scores, axis=0, keepdims=True)
        powers = jnp.exp2(scores - top)
        weights = powers * (1.0 / jnp.sum(powers, axis=0, keepdims=True))
        low = weights.astype(jnp.bfloat16)
        grad_weights = lax.dot_general(values, do, contract, preferred_element_type=jnp.float32)
        row_dot = jnp.sum(weights * grad_weights, axis=0, keepdims=True)
        score_grad = (weights * (grad_weights - row_dot) * scale).astype(jnp.bfloat16)
        values_t = jnp.concatenate([vt[e] for e in at], axis=1)
        keys_t = jnp.concatenate([kt[e] for e in at], axis=1)
        out_t = jnp.dot(values_t, low, preferred_element_type=jnp.float32)
        dq_t = jnp.dot(keys_t, score_grad, preferred_element_type=jnp.float32)
        outx[:, columns] = out_t.T.astype(jnp.bfloat16)
        dqx[:, columns] = dq_t.T.astype(jnp.bfloat16)
        dv = jnp.dot(low, do, preferred_element_type=jnp.float32)
        dk = jnp.dot(score_grad, q, preferred_element_type=jnp.float32)
        for t, e in enumerate(at):
            kacc[e] += dk[t * BLOCK:(t + 1) * BLOCK]
            vacc[e] += dv[t * BLOCK:(t + 1) * BLOCK]

    def head_step(h, carry):
        head = g * heads + h
        shard, local = head // per_shard, head % per_shard
        count = jnp.int32(1)
        names[0] = block
        for t in range(1, list_len):
            entry = table[shard, local, block * list_len + t]
            names[count] = entry
            count = count + jnp.where(entry < blocks, 1, 0).astype(jnp.int32)
        columns = pl.ds(pl.multiple_of(h * HEAD_SIZE, HEAD_SIZE), HEAD_SIZE)
        for n in range(1, list_len + 1):
            pl.when(count == n)(functools.partial(work, n, columns))
        return carry

    lax.fori_loop(0, heads, head_step, 0)

    def finish(j, carry):
        gk[j] = kacc[j].astype(jnp.bfloat16)
        gv[j] = vacc[j].astype(jnp.bfloat16)
        return carry

    lax.fori_loop(0, blocks, finish, 0)


def scatter_kernel(
    width, chips,
    outx, dqx, gk, gv,
    out, dq, out_k, out_v,
    rk, rv, ak, av, fk, fv,
    ks, kr, vs, vr, ps, pr,
):
    u, b = lax.axis_index("uly"), lax.axis_index("blk")
    c, g = b // 2, b % 2
    half = outx.shape[1]
    seg = out.shape[0]
    mine = pl.ds(pl.multiple_of(g * seg, seg), seg)
    theirs = pl.ds(pl.multiple_of((1 - g) * seg, seg), seg)
    my_head = pl.ds(pl.multiple_of(g * HEAD_SIZE, HEAD_SIZE), HEAD_SIZE)
    my_half = pl.ds(pl.multiple_of(g * half, half), half)
    sibling = (u, c * 2 + (1 - g))
    greet(width, chips, u, b, c, g)
    started = []

    def start(copy, needed=None):
        if needed is None:
            copy.start()
        else:
            pl.when(needed)(copy.start)
        started.append((copy, needed))
        return copy

    def place(m, d):
        return flip(u, m, width) * chips + (c + d) % chips

    orders = (bits_of(width)[::-1], bits_of(width))
    arrays = ((gk, rk, ak, ks, kr), (gv, rv, av, vs, vr))
    stages = len(orders[0])
    bases = []
    total = 0
    for t in range(stages):
        bases.append(total)
        total += (width >> (t + 1)) * chips
    line = total
    ranked = [
        [sorted(span(order[t + 1:]), key=lambda m: -bin(m).count("1")) for t in range(stages)]
        for order in orders
    ]

    def slot(which, t, s, d):
        return bases[t] + ranked[which][t].index(s) * chips + d

    def current(which, t, m, d):
        grads, _, sums, _, _ = arrays[which]
        if t == 0:
            return grads.at[place(m, d)]
        return sums.at[slot(which, t - 1, m, d)]

    def send(which, t, s, d):
        _, landing, _, ssem, rsem = arrays[which]
        bit = orders[which][t]
        at = slot(which, t, s, d)
        start(
            remote(
                current(which, t, s ^ bit, d), landing.at[at], ssem.at[at], rsem.at[at],
                (flip(u, bit, width), b),
            ),
            place(s ^ bit, d) <= top(u, orders[which][:t]) * chips + c,
        )

    def receive(which, at, needed):
        _, landing, _, ssem, rsem = arrays[which]
        copy = remote(landing.at[at], landing.at[at], ssem.at[at], rsem.at[at], sibling)
        pl.when(needed)(copy.wait_recv)

        @pl.when(jnp.logical_not(needed))
        def _():
            landing[at] = jnp.zeros((BLOCK, HEAD_SIZE), landing.dtype)

    line_order = list(range(1, chips)) + [0]
    for t_s in range(width // 2):
        for d in line_order:
            for which in (0, 1):
                send(which, 0, ranked[which][0][t_s], d)
    pair = [
        start(remote(outx.at[theirs, :], out.at[:, my_half], ps.at[0], pr.at[0], sibling)),
        start(remote(dqx.at[theirs, :], dq.at[:, my_half], ps.at[1], pr.at[1], sibling)),
    ]
    out[:, my_half] = outx[mine, :]
    dq[:, my_half] = dqx[mine, :]

    for t in range(stages):
        for s_at in range(len(ranked[0][t])):
            for d in line_order:
                for which in (0, 1):
                    _, landing, sums, ssem, rsem = arrays[which]
                    s = ranked[which][t][s_at]
                    at = slot(which, t, s, d)
                    u_there = flip(u, orders[which][t], width)
                    reach = top(u_there, orders[which][:t]) * chips + c
                    receive(which, at, place(s, d) <= reach)
                    own = current(which, t, s, d)
                    sums[at] = (
                        own[...].astype(jnp.float32) + landing[at].astype(jnp.float32)
                    ).astype(jnp.bfloat16)
                    if t + 1 < stages:
                        if s & orders[which][t + 1]:
                            send(which, t + 1, s ^ orders[which][t + 1], d)
                    elif d:
                        start(
                            remote(
                                sums.at[at], landing.at[line + (chips - d) % chips],
                                ssem.at[line + d], rsem.at[line + (chips - d) % chips],
                                (u, ((c + d) % chips) * 2 + g),
                            ),
                            place(0, d) <= (width - 1) * chips + c,
                        )
    finals = ((fk, out_k), (fv, out_v))
    last = []
    for which in (0, 1):
        _, landing, sums, ssem, rsem = arrays[which]
        result, target = finals[which]
        value = sums[slot(which, stages - 1, 0, 0)].astype(jnp.float32)
        for d in range(1, chips):
            at = line + d
            receive(which, at, u * chips + c <= (width - 1) * chips + (c + d) % chips)
            value = value + landing[at].astype(jnp.float32)
        result[...] = value.astype(jnp.bfloat16)
        last.append(start(remote(
            result.at[theirs, :], target.at[:, my_head], ps.at[2 + which], pr.at[2 + which], sibling
        )))
        target[:, my_head] = result[mine, :]
    for copy in pair + last:
        copy.wait_recv()
    for copy, needed in started:
        if needed is None:
            copy.wait_send()
        else:
            pl.when(needed)(copy.wait_send)


def body(queries, key_rows, value_rows, out_grad, block_list):
    width = lax.axis_size("uly")
    chips = lax.axis_size("blk") // 2
    seg, columns = queries.shape
    heads_dev, blocks, list_len = block_list.shape
    heads = heads_dev * width // KEY_VALUE_HEADS
    half = columns // 2
    low = jnp.bfloat16
    vmem = pl.BlockSpec(memory_space=pltpu.VMEM)
    smem = pl.BlockSpec(memory_space=pltpu.SMEM)
    dma = pltpu.SemaphoreType.DMA

    earlier = jnp.arange(list_len)[:, None] > jnp.arange(list_len)[None, :]
    repeated = jnp.any(
        (block_list[:, :, :, None] == block_list[:, :, None, :]) & earlier[None, None], axis=3
    )
    lists = jnp.where(repeated, blocks, block_list).reshape(heads_dev, blocks * list_len)

    cube = jax.ShapeDtypeStruct((blocks, BLOCK, HEAD_SIZE), low)
    wide = jax.ShapeDtypeStruct((BLOCK, half), low)
    qx, dox, kall, vall, kt, vt, table = pl.pallas_call(
        functools.partial(gather_kernel, width, chips),
        out_shape=(
            wide, wide, cube, cube, cube, cube,
            jax.ShapeDtypeStruct((width, heads_dev, blocks * list_len), jnp.int32),
        ),
        in_specs=[vmem] * 5,
        out_specs=(vmem,) * 7,
        scratch_shapes=[dma((width * chips,))] * 4 + [dma((width,))] * 2 + [dma((4,))] * 2,
        compiler_params=pltpu.CompilerParams(
            collective_id=0, has_side_effects=True, vmem_limit_bytes=VMEM_LIMIT
        ),
        name="gather",
    )(queries, out_grad, key_rows, value_rows, lists)

    outx, dqx, gk, gv = pl.pallas_call(
        functools.partial(attention_kernel, chips, heads, list_len),
        out_shape=(wide, wide, cube, cube),
        in_specs=[smem] + [vmem] * 6,
        out_specs=(vmem,) * 4,
        scratch_shapes=[
            pltpu.SMEM((list_len + 1,), jnp.int32),
            pltpu.VMEM((blocks, BLOCK, HEAD_SIZE), jnp.float32),
            pltpu.VMEM((blocks, BLOCK, HEAD_SIZE), jnp.float32),
        ],
        compiler_params=pltpu.CompilerParams(vmem_limit_bytes=VMEM_LIMIT),
        name="attention",
    )(table, qx, dox, kall, vall, kt, vt)

    slots = width * chips
    landing = pltpu.VMEM((slots, BLOCK, HEAD_SIZE), low)
    return pl.pallas_call(
        functools.partial(scatter_kernel, width, chips),
        out_shape=(
            jax.ShapeDtypeStruct((seg, columns), low),
            jax.ShapeDtypeStruct((seg, columns), low),
            jax.ShapeDtypeStruct((seg, KEY_VALUE_HEADS * HEAD_SIZE), low),
            jax.ShapeDtypeStruct((seg, KEY_VALUE_HEADS * HEAD_SIZE), low),
        ),
        in_specs=[vmem] * 4,
        out_specs=(vmem,) * 4,
        scratch_shapes=[landing] * 4
        + [pltpu.VMEM((BLOCK, HEAD_SIZE), low)] * 2
        + [dma((slots,))] * 4
        + [dma((4,))] * 2,
        compiler_params=pltpu.CompilerParams(
            collective_id=1, has_side_effects=True, vmem_limit_bytes=VMEM_LIMIT
        ),
        name="scatter",
    )(outx, dqx, gk, gv)


def solution(mesh):
    rows = P(("uly", "blk"), None)
    return jax.shard_map(
        body,
        mesh=mesh,
        in_specs=(rows, rows, rows, rows, P("uly", None, None)),
        out_specs=(rows, rows, rows, rows),
        check_vma=False,
    )
```
